32 devices in a mesh: group: 2 (over x), expert: 16 (over z, y, core), tensor: 1.
Axes of the slice: x: 2, y: 2, z: 4, core: 2. Of those that a mesh axis runs over, the one named last changes fastest.
Arguments:
- tokens: bfloat16 [4096, 3584], P(('group', 'expert'), 'tensor'), parts along dimension 0, may hold values from -6 to 6
- routes: int32 [4096, 8], P(('group', 'expert')), parts along dimension 0, may hold values from 0 to 16, all different within a row; in each aligned block of 128 rows (0 to 127, 128 to 255, ...) at most 64 rows name the same one
- gate_q: int32 [4096, 8], P(('group', 'expert')), parts along dimension 0, may hold values from 1 to 255
- hot_list: int32 [1], replicated, may hold values from 0 to 16
- cold_gate_up: bfloat16 [16, 2, 3584, 1024], P('expert', None, None, 'tensor'), may hold values from -0.09375 to 0.09375
- cold_down: bfloat16 [16, 1024, 3584], P('expert', 'tensor'), may hold values from -0.1875 to 0.1875
- hot_gate_up: bfloat16 [1, 2, 3584, 1024], P(None, None, None, 'tensor'), may hold values from -0.09375 to 0.09375
- hot_down: bfloat16 [1, 1024, 3584], P(None, 'tensor'), may hold values from -0.1875 to 0.1875
Outputs:
- mixed: bfloat16 [4096, 3584], P(('group', 'expert'), 'tensor'), parts along dimension 0
The draws below stay inside these ranges and needn't reach their ends.
There are 2 independent parts, one for each index of `group`. The reference program is written for one: setup_inputs(seed, part) draws one part's arguments, and reference() takes and returns one part's arrays. A program takes and returns all parts, laid end to end along the dimension named above; an argument that names none is the same for every part. Nothing has to cross between parts.
Inputs may be any that keep to these rules, and one draw needn't show every extreme that they name: `routes`: each row names 8 distinct experts; within the 128 rows of one index of expert, no expert is named by more than 64 rows, a bound that some block reaches. `hot_list`: the hot ids are distinct.
All inputs are finite; a program needn't handle non-finite values.
Results may differ from the reference program's by a relative error of at most 0.0065.
Values may be sent and summed in bfloat16 or wider, within the bound.
A program may use at most 128 MiB of HBM per device.

```python
import math
import jax
import jax.numpy as jnp
import numpy as np
from jax import lax

D = 3584
F = 1024
TOP = 8
HOT = 1
ROW_DEV = 128
ROWS = 2048
EXPERTS = 17
CAP = 64
N_EXPERT = 16


def touch_ends(result, rng, low, largest):
    place = [jax.random.randint(jax.random.fold_in(rng, axis), (), 0, length) for axis, length in enumerate(result.shape)]
    widest = result.shape.index(max(result.shape))
    next_to = place[:widest] + [(place[widest] + 1) % result.shape[widest]] + place[widest + 1:]
    return result.at[tuple(place)].set(low).at[tuple(next_to)].set(largest)


def level_of(rng, extent, split, least, top_value):
    def one(dim, shards_of):
        draws = jax.random.uniform(jax.random.fold_in(jax.random.fold_in(rng, 6), dim), (shards_of,), jnp.float32, least / len(split), top_value / len(split))
        return jnp.repeat(jnp.exp(draws), extent[dim] // shards_of).reshape((-1,) + (1,) * (len(extent) - dim - 1))

    factor_of = one(*split[0])
    for cut in split[1:]:
        factor_of = factor_of * one(*cut)
    return factor_of


def shared_out(stream_key, own, number, rows, count, top, limit, slope):
    sequence = jax.random.permutation(stream_key, count)
    crowded, usual = portions_of(count, rows * top, limit, slope, True), portions_of(count, rows * top, limit, slope, False)
    places = jnp.arange(count)

    def named(lengths, offset_by):
        used = int((lengths > 0).sum())
        fixed = max(1, used // 4)
        moved = fixed + (places - fixed + offset_by * (used - fixed)) % max(1, count - fixed)
        return jnp.zeros((count,), jnp.int32).at[sequence[jnp.where(places < fixed, places, moved)]].set(jnp.asarray(lengths, jnp.int32))

    lengths = jnp.where(number % 4 == 0, named(crowded, number // 4), named(usual, number - number // 4 - 1))
    mixed = jax.random.permutation(jax.random.fold_in(own, 3), count)
    source_of, receiver = mixed[0:count // 2 * 2:2], mixed[1:count // 2 * 2:2]
    room = jnp.minimum(lengths[source_of] - 1, limit - lengths[receiver]) // 2
    room = jnp.where((source_of == sequence[0]) | (receiver == sequence[0]) | (lengths[receiver] == 0), 0, jnp.maximum(room, 0))
    moved = jax.random.randint(jax.random.fold_in(own, 4), (count // 2,), 0, 1 << 20) % (room + 1)
    lengths = lengths.at[source_of].add(-moved).at[receiver].add(moved)
    items = jnp.searchsorted(jnp.cumsum(lengths), jnp.arange(rows * top), side="right").astype(jnp.int32)
    listing = items.reshape(top, rows).T
    listing = listing[jax.random.permutation(jax.random.fold_in(own, 1), rows)]
    offset_by = jax.random.randint(jax.random.fold_in(own, 2), (rows, 1), 0, top)
    return jnp.take_along_axis(listing, (jnp.arange(top)[None, :] + offset_by) % top, axis=1)


def portions_of(amount, total, reach, skew, full):
    portions = [(1 << 20) // math.isqrt(standing ** skew) + 1 for standing in range(1, amount + 1)]
    largest = reach if full else min(reach, max(-(-total // amount), total * portions[0] // sum(portions)))
    least = 1 if total - largest >= amount - 1 else 0
    holding, surplus = [largest] + [least] * (amount - 1), total - largest - least * (amount - 1)
    while surplus > 0:
        candidates = [i for i in range(1, amount) if holding[i] < largest] or [i for i in range(1, amount) if holding[i] < reach]
        whole, left = sum([portions[i] for i in candidates]), surplus
        for i in candidates:
            extra = min(reach - holding[i], max(1, left * portions[i] // whole), surplus)
            holding[i] = holding[i] + extra
            surplus = surplus - extra
    return np.array(holding)


def centred(own_key, shape, spread, reach, pieces=(), kind=jnp.bfloat16):
    result = jax.random.normal(own_key, shape, jnp.float32) * spread
    if len(pieces) > 0:
        result = level_of(own_key, shape, pieces, -0.22, 0.18) * result
    return jnp.clip(result, min=-reach, max=reach).astype(kind)


def setup_inputs(seed: int = 0, part: int = 0) -> dict:
    keys = jax.random.split(jax.random.key(seed), 9)
    part_splits = jax.random.split(jax.random.fold_in(keys[8], part), 9)
    tokens = centred(part_splits[0], (ROWS, D), 1.0, 6.0, ((0, 16),))
    routes_keys = jax.random.split(jax.random.fold_in(part_splits[1], 1), ROWS // ROW_DEV)
    routes_turns = jax.random.permutation(jax.random.fold_in(part_splits[1], 3), ROWS // ROW_DEV)
    routes = jax.vmap(lambda own, number: shared_out(jax.random.fold_in(part_splits[1], 2), own, number, ROW_DEV, EXPERTS, TOP, CAP, 2))(routes_keys, routes_turns).reshape((ROWS, TOP))
    gate_q = touch_ends(jax.random.randint(part_splits[2], (ROWS, TOP), 1, 256), jax.random.fold_in(part_splits[2], 1), 1, 255).astype(jnp.int32)
    hot_list = jax.random.randint(keys[3], (HOT,), 0, EXPERTS).astype(jnp.int32)
    cold_gate_up = centred(keys[4], (N_EXPERT, 2, D, F), D ** -0.5, 0.09375, ((0, 16),))
    cold_down = centred(keys[5], (N_EXPERT, F, D), F ** -0.5, 0.1875, ((0, 16),))
    hot_gate_up = centred(keys[6], (HOT, 2, D, F), D ** -0.5, 0.09375)
    hot_down = centred(keys[7], (HOT, F, D), F ** -0.5, 0.1875)
    return dict(tokens=tokens, routes=routes, gate_q=gate_q, hot_list=hot_list, cold_gate_up=cold_gate_up, cold_down=cold_down, hot_gate_up=hot_gate_up, hot_down=hot_down)


def slot_table(hot_list, experts_all):
    labels = jnp.arange(experts_all, dtype=jnp.int32)
    hot_match = (hot_list[:, None] == labels[None, :]).astype(jnp.int32)
    is_hot = jnp.sum(hot_match, axis=0)
    cold_rank = jnp.cumsum(1 - is_hot) - 1
    return is_hot, cold_rank, hot_match


def route_weights(routes, gate_q, experts_all):
    quantized = gate_q.astype(jnp.float32)
    shares = quantized / jnp.sum(quantized, axis=1, keepdims=True)
    labels = jnp.arange(experts_all, dtype=jnp.int32)
    picked = routes[:, :, None] == labels[None, None, :]
    chosen = jnp.sum(picked.astype(jnp.int32), axis=1)
    weight = jnp.sum(jnp.where(picked, shares[:, :, None], jnp.float32(0.0)), axis=1)
    return chosen, weight


def expert_rows(inputs, gate_up, down_proj):
    paired = jnp.einsum('nd,gdf->gnf', inputs.astype(jnp.float32), gate_up.astype(jnp.float32))
    hidden = (jax.nn.silu(paired[0]) * paired[1]).astype(jnp.bfloat16)
    return jnp.einsum('nf,fd->nd', hidden.astype(jnp.float32), down_proj.astype(jnp.float32)).astype(jnp.bfloat16)


def reference(tokens, routes, gate_q, hot_list, cold_gate_up, cold_down, hot_gate_up, hot_down):
    experts_all = N_EXPERT + HOT
    is_hot, cold_rank, hot_match = slot_table(hot_list, experts_all)
    chosen, weight = route_weights(routes, gate_q, experts_all)
    labels = jnp.arange(experts_all, dtype=jnp.int32)
    cold_label = jnp.sum(labels[None, :] * ((cold_rank[None, :] == jnp.arange(N_EXPERT, dtype=jnp.int32)[:, None]) & (is_hot[None, :] == 0)).astype(jnp.int32), axis=1).astype(jnp.int32)
    blocked = chosen.reshape(N_EXPERT, ROW_DEV, experts_all)
    placed = (jnp.cumsum(blocked, axis=1) - 1).reshape(ROWS, experts_all)
    block_start = (jnp.arange(ROWS, dtype=jnp.int32) // ROW_DEV) * CAP
    destination = block_start[:, None] + placed
    row_index = jnp.arange(ROWS, dtype=jnp.int32)
    padded = N_EXPERT * CAP

    def contribute(total_out, label, gate_up, down_proj):
        hit = jnp.take(chosen, label, axis=1) > 0
        where_to = jnp.where(hit, jnp.take(destination, label, axis=1), padded).astype(jnp.int32)
        row_ids = jnp.zeros((padded,), jnp.int32).at[where_to].set(row_index, mode='drop')
        valid = jnp.zeros((padded,), jnp.float32).at[where_to].set(jnp.take(weight, label, axis=1), mode='drop')
        results = expert_rows(tokens[row_ids], gate_up, down_proj)
        return total_out.at[row_ids].add(valid[:, None] * results.astype(jnp.float32))

    def cold_step(total_out, packed):
        label, gate_up, down_proj = packed
        return contribute(total_out, label, gate_up, down_proj), None

    total_out = jnp.zeros((ROWS, D), jnp.float32)
    total_out, unused = lax.scan(cold_step, total_out, (cold_label, cold_gate_up, cold_down))
    for position in range(HOT):
        total_out = contribute(total_out, hot_list[position].astype(jnp.int32), hot_gate_up[position], hot_down[position])
    return total_out.astype(jnp.bfloat16)
```

```python
import functools

import jax
import jax.numpy as jnp
from jax import lax
from jax.experimental import pallas as pl
from jax.experimental.pallas import tpu as pltpu
from jax.sharding import PartitionSpec as P

TOP = 8
HOT = 1
NZ, NY, NC = 4, 2, 2
LANES = 128
F32 = jnp.float32
BF16 = jnp.bfloat16


def place():
    e = lax.axis_index("expert")
    return e // (NY * NC), (e // NC) % NY, e % NC


def index(z, y, c):
    return (z * NY + y) * NC + c


def greet(z, y, c):
    barrier = pltpu.get_barrier_semaphore()

    def hello(dev):
        pl.semaphore_signal(
            barrier, inc=1, device_id={"expert": dev}, device_id_type=pl.DeviceIdType.MESH
        )

    hello(index(z, y, 1 - c))
    hello(index(z, 1 - y, c))

    @pl.when(z > 0)
    def _():
        hello(index(z - 1, y, c))

    @pl.when(z < NZ - 1)
    def _():
        hello(index(z + 1, y, c))

    ends = (z == 0) | (z == NZ - 1)

    @pl.when(ends)
    def _():
        pl.semaphore_wait(barrier, 3)

    @pl.when(jnp.logical_not(ends))
    def _():
        pl.semaphore_wait(barrier, 4)


def spread_kernel(first, x_ref, out_ref, own_sem, send_sem, recv_sem):
    z, y, c = place()
    rows = x_ref.shape[0]
    parts = (pl.ds(0, first), pl.ds(first, rows - first))
    up, down, side, core = 0, 1, 2, 3
    own = index(z, y, c)
    keep = pltpu.make_async_copy(x_ref, out_ref.at[own], own_sem)
    keep.start()
    greet(z, y, c)

    def copy(way, source, part, from_input=False):
        target = (index(z + 1, y, c), index(z - 1, y, c), index(z, 1 - y, c), index(z, y, 1 - c))[way]
        block = x_ref if from_input else out_ref.at[source]
        return pltpu.make_async_remote_copy(
            src_ref=block.at[parts[part]],
            dst_ref=out_ref.at[source, parts[part]],
            send_sem=send_sem.at[way, source, part],
            recv_sem=recv_sem.at[source, part],
            device_id={"expert": target},
            device_id_type=pl.DeviceIdType.MESH,
        )

    def send(way, source, part, go=None, from_input=False):
        if go is None:
            copy(way, source, part, from_input).start()
        else:
            pl.when(go)(lambda: copy(way, source, part, from_input).start())

    def arrived(source, part):
        copy(core, source, part).wait_recv()

    def sent(way, source, part, go=None):
        if go is None:
            copy(way, source, part).wait_send()
        else:
            pl.when(go)(lambda: copy(way, source, part).wait_send())

    has_up, has_down = z < NZ - 1, z > 0
    beside = index(z, 1 - y, c)
    for part in (1, 0):
        send(up, own, part, has_up, True)
        send(down, own, part, has_down, True)
        send(side, own, part, None, True)
    for part in (0, 1):
        send(core, own, part, None, True)
    arrived(beside, 1)
    send(up, beside, 1, has_up)
    send(down, beside, 1, has_down)
    send(core, beside, 1)

    def step(k, finish):
        for way in (up, down):
            zs = z - k if way == up else z + k
            there = (zs >= 0) if way == up else (zs < NZ)
            onward = has_up if way == up else has_down

            @pl.when(there)
            def _():
                mine, other = index(zs, y, c), index(zs, 1 - y, c)
                order = ((mine, 1), (mine, 0), (other, 1))
                for source, part in order:
                    if finish:
                        sent(way, source, part, onward)
                        sent(core, source, part)
                    else:
                        arrived(source, part)
                        send(way, source, part, onward)
                        if part == 0:
                            send(side, source, part)
                        send(core, source, part)
                if finish:
                    sent(side, mine, 0)

    def cross(k, finish):
        for zs, there in ((z - k, z - k >= 0), (z + k, z + k < NZ)):

            @pl.when(there)
            def _():
                other = index(zs, 1 - y, c)
                if finish:
                    sent(core, other, 0)
                else:
                    arrived(other, 0)
                    send(core, other, 0)

    for k in range(1, NZ):
        step(k, False)
        if k == 1:
            arrived(beside, 0)
            send(core, beside, 0)
        else:
            cross(k - 1, False)
    cross(NZ - 1, False)
    for zs in range(NZ):
        for ys in range(NY):
            for part in (0, 1):
                arrived(index(zs, ys, 1 - c), part)
    for part in (1, 0):
        sent(up, own, part, has_up)
        sent(down, own, part, has_down)
        sent(side, own, part)
        sent(core, own, part)
        sent(core, beside, part)
    sent(up, beside, 1, has_up)
    sent(down, beside, 1, has_down)
    for k in range(1, NZ):
        step(k, True)
        cross(k, True)
    keep.wait()


def spread(x, first):
    n = NZ * NY * NC
    return pl.pallas_call(
        functools.partial(spread_kernel, first),
        out_shape=jax.ShapeDtypeStruct((n,) + x.shape, x.dtype),
        in_specs=[pl.BlockSpec(memory_space=pl.ANY)],
        out_specs=pl.BlockSpec(memory_space=pl.ANY),
        scratch_shapes=[
            pltpu.SemaphoreType.DMA,
            pltpu.SemaphoreType.DMA((4, n, 2)),
            pltpu.SemaphoreType.DMA((n, 2)),
        ],
        compiler_params=pltpu.CompilerParams(collective_id=0, has_side_effects=True),
    )(x)


def fold_kernel(
    first, p_ref, hot_ref, o_ref, core_in, side_a, side_b, line_a, line_b, out_ya, out_yb, out_za, out_zb,
    core_s, core_r, ya_s, ya_r, yb_s, yb_r, za_s, za_r, zb_s, zb_r,
):
    z, y, c = place()
    rows = o_ref.shape[0]
    part_a, part_b = (0, first), (first, rows - first)
    greet(z, y, c)

    def remote(src, dst, s, r, target):
        return pltpu.make_async_remote_copy(
            src_ref=src, dst_ref=dst, send_sem=s, recv_sem=r,
            device_id={"expert": target}, device_id_type=pl.DeviceIdType.MESH,
        )

    def core_copy(zd, yd):
        return remote(p_ref.at[index(zd, yd, 1 - c)], core_in.at[zd, yd], core_s.at[zd, yd], core_r.at[zd, yd], index(z, y, 1 - c))

    def ya_copy(zd):
        return remote(out_ya.at[zd], side_a.at[zd], ya_s.at[zd], ya_r.at[zd], index(z, 1 - y, c))

    def yb_copy():
        return remote(out_yb, side_b, yb_s, yb_r, index(z, 1 - y, c))

    def za_copy(way, zd):
        return remote(out_za.at[zd], line_a.at[way, zd], za_s.at[zd], za_r.at[way, zd], index(z + 1 - 2 * way, y, c))

    def zb_copy(way, zd, yd):
        return remote(out_zb.at[zd, yd], line_b.at[way, zd, yd], zb_s.at[zd, yd], zb_r.at[way, zd, yd], index(z + 1 - 2 * way, y, c))

    def add(dst, part, *sources):
        def one(i, carry):
            at = pl.multiple_of(i * 16, 16)
            total = sources[0][0][pl.ds(sources[0][1] + at, 16), :].astype(F32)
            for ref, start in sources[1:]:
                total = total + ref[pl.ds(start + at, 16), :].astype(F32)
            dst[0][pl.ds(dst[1] + at, 16), :] = total.astype(dst[0].dtype)
            return carry

        lax.fori_loop(0, part[1] // 16, one, 0)

    def each(k, f):
        if k == 0:
            f(z, None)
        else:
            pl.when(z + k < NZ)(lambda: f(z + k, 0))
            pl.when(z - k >= 0)(lambda: f(z - k, 1))

    def start_core(zd, way):
        for yd in range(NY):
            core_copy(zd, yd).start()

    def over_core(zd, way):
        core_copy(zd, 1 - y).wait_recv()
        add((out_ya.at[zd], 0), part_a, (p_ref.at[index(zd, 1 - y, c)], 0), (core_in.at[zd, 1 - y], 0))
        ya_copy(zd).start()
        core_copy(zd, y).wait_recv()

    def along(zd, way):
        first_of_line = (z == 0) if way == 0 else (z == NZ - 1)

        for yd in range(NY):
            base = ((p_ref.at[index(zd, yd, c)], first), (core_in.at[zd, yd], first))

            @pl.when(first_of_line)
            def _():
                add((out_zb.at[zd, yd], 0), part_b, *base)

            @pl.when(jnp.logical_not(first_of_line))
            def _():
                zb_copy(way, zd, yd).wait_recv()
                add((out_zb.at[zd, yd], 0), part_b, *base, (line_b.at[way, zd, yd], 0))

            zb_copy(way, zd, yd).start()
        ya_copy(zd).wait_recv()
        base = ((p_ref.at[index(zd, y, c)], 0), (core_in.at[zd, y], 0), (side_a.at[zd], 0))

        @pl.when(first_of_line)
        def _():
            add((out_za.at[zd], 0), part_a, *base)

        @pl.when(jnp.logical_not(first_of_line))
        def _():
            za_copy(way, zd).wait_recv()
            add((out_za.at[zd], 0), part_a, *base, (line_a.at[way, zd], 0))

        za_copy(way, zd).start()

    def finish(zd):
        def by_end(f):
            pl.when(z == 0)(lambda: f((1,)))
            pl.when(z == NZ - 1)(lambda: f((0,)))
            pl.when((z > 0) & (z < NZ - 1))(lambda: f((0, 1)))

        def last_b(ways):
            for yd, dst in ((1 - y, out_yb), (y, None)):
                for way in ways:
                    zb_copy(way, zd, yd).wait_recv()
                base = ((p_ref.at[index(zd, yd, c)], first), (core_in.at[zd, yd], first)) + tuple(
                    (line_b.at[way, zd, yd], 0) for way in ways
                )
                if dst is None:
                    yb_copy().wait_recv()
                    add((o_ref, first), part_b, *base, (side_b, 0), (hot_ref, first))
                else:
                    add((dst, 0), part_b, *base)
                    yb_copy().start()

        def last_a(ways):
            for way in ways:
                za_copy(way, zd).wait_recv()
            add(
                (o_ref, 0), part_a, (p_ref.at[index(zd, y, c)], 0), (core_in.at[zd, y], 0), (side_a.at[zd], 0),
                (hot_ref, 0), *((line_a.at[way, zd], 0) for way in ways),
            )

        ya_copy(zd).wait_recv()
        by_end(last_b)
        by_end(last_a)

    def drain(zd, way):
        for yd in range(NY):
            core_copy(zd, yd).wait_send()
        ya_copy(zd).wait_send()
        if way is None:
            yb_copy().wait_send()
        else:
            za_copy(way, zd).wait_send()
            for yd in range(NY):
                zb_copy(way, zd, yd).wait_send()

    for k in (3, 2, 1, 0):
        each(k, start_core)
    each(3, over_core)
    each(2, over_core)
    each(3, along)
    each(1, over_core)
    each(2, along)
    each(0, over_core)
    each(1, along)
    finish(z)
    for k in (3, 2, 1, 0):
        each(k, drain)


def fold(parts, hot, first):
    n, rows, width = parts.shape
    rest = rows - first
    dma = pltpu.SemaphoreType.DMA
    return pl.pallas_call(
        functools.partial(fold_kernel, first),
        out_shape=jax.ShapeDtypeStruct((rows, width), BF16),
        in_specs=[pl.BlockSpec(memory_space=pltpu.VMEM)] * 2,
        out_specs=pl.BlockSpec(memory_space=pltpu.VMEM),
        scratch_shapes=[
            pltpu.VMEM((NZ, NY, rows, width), BF16),
            pltpu.VMEM((NZ, first, width), BF16),
            pltpu.VMEM((rest, width), BF16),
            pltpu.VMEM((2, NZ, first, width), BF16),
            pltpu.VMEM((2, NZ, NY, rest, width), BF16),
            pltpu.VMEM((NZ, first, width), BF16),
            pltpu.VMEM((rest, width), BF16),
            pltpu.VMEM((NZ, first, width), BF16),
            pltpu.VMEM((NZ, NY, rest, width), BF16),
            dma((NZ, NY)), dma((NZ, NY)),
            dma((NZ,)), dma((NZ,)),
            dma, dma,
            dma((NZ,)), dma((2, NZ)),
            dma((NZ, NY)), dma((2, NZ, NY)),
        ],
        compiler_params=pltpu.CompilerParams(
            collective_id=1, has_side_effects=True, vmem_limit_bytes=60 * 2**20
        ),
    )(parts, hot)


def meshed(tokens, routes, gate_q, hot_list, cold_gate_up, cold_down, hot_gate_up, hot_down):
    n = lax.axis_size("expert")
    rows, width = tokens.shape
    capacity = rows * TOP // n
    first = rows - 16
    is_hot, cold_rank, hot_match = slot_table(hot_list, n + HOT)
    picked = routes[:, :, None] == jnp.arange(n + HOT, dtype=jnp.int32)[None, None, :]
    by_label = jnp.sum(jnp.where(picked, gate_q[:, :, None], 0), axis=1)
    to_slot = jnp.where(is_hot > 0, n, cold_rank)
    slot_of = to_slot[:, None] == jnp.arange(n + 1, dtype=jnp.int32)[None, :]
    by_slot = jnp.sum(jnp.where(slot_of[None], by_label[:, :, None], 0), axis=1)
    whole = jnp.sum(gate_q, axis=1, keepdims=True)
    extra = jnp.concatenate([by_slot[:, :n], whole // 256, whole % 256], axis=1).astype(BF16)
    extra = jnp.pad(extra, ((0, 0), (0, LANES - extra.shape[1])))
    everything = spread(jnp.concatenate([tokens, extra], axis=1), first)

    notes = everything[:, :, width:].astype(F32)
    slot = lax.axis_index("expert")
    gate = jnp.sum(jnp.where(jnp.arange(LANES) == slot, notes, 0.0), axis=2)
    total = notes[:, :, n] * 256.0 + notes[:, :, n + 1]
    share = gate / total
    taken = gate > 0
    rank = jnp.cumsum(taken.astype(jnp.int32), axis=1) - 1
    hit = (rank[:, :, None] == jnp.arange(capacity, dtype=jnp.int32)) & taken[:, :, None]
    hit = hit.astype(BF16)
    x = jnp.einsum("brc,brd->bcd", hit, everything[:, :, :width], preferred_element_type=F32)
    x = x.astype(BF16).reshape(n * capacity, width)
    answers = expert(x, cold_gate_up[0], cold_down[0]).reshape(n, capacity, width)
    part = jnp.einsum("brc,bcd->brd", hit, answers, preferred_element_type=F32)
    part = (part * share[:, :, None]).astype(BF16)

    hot_share = by_slot[:, n:].astype(F32) / whole.astype(F32)
    hot = hot_share * expert(tokens, hot_gate_up[0], hot_down[0]).astype(F32)
    return fold(part, hot, first)


def expert(x, gate_up, down):
    paired = jnp.einsum("nd,gdf->gnf", x, gate_up, preferred_element_type=F32)
    hidden = (jax.nn.silu(paired[0]) * paired[1]).astype(BF16)
    return jnp.einsum("nf,fd->nd", hidden, down, preferred_element_type=F32).astype(BF16)


def slot_table(hot_list, experts_all):
    labels = jnp.arange(experts_all, dtype=jnp.int32)
    hot_match = (hot_list[:, None] == labels[None, :]).astype(jnp.int32)
    is_hot = jnp.sum(hot_match, axis=0)
    cold_rank = jnp.cumsum(1 - is_hot) - 1
    return (is_hot, cold_rank, hot_match)


def route_weights(routes, gate_q, experts_all):
    quantized = gate_q.astype(jnp.float32)
    shares = quantized / jnp.sum(quantized, axis=1, keepdims=True)
    labels = jnp.arange(experts_all, dtype=jnp.int32)
    picked = routes[:, :, None] == labels[None, None, :]
    chosen = jnp.sum(picked.astype(jnp.int32), axis=1)
    weight = jnp.sum(jnp.where(picked, shares[:, :, None], jnp.float32(0.0)), axis=1)
    return (chosen, weight, shares)


def swiglu(inputs, gate_up, down_proj):
    paired = jnp.einsum("snd,gdf->gsnf", inputs, gate_up, preferred_element_type=jnp.float32)
    hidden = (jax.nn.silu(paired[0]) * paired[1]).astype(jnp.bfloat16)
    return jnp.einsum("snf,fd->snd", hidden, down_proj, preferred_element_type=jnp.float32)


def local(tokens, routes, gate_q, hot_list, cold_gate_up, cold_down, hot_gate_up, hot_down):
    experts_cold = lax.axis_size("expert")
    experts_all = experts_cold + HOT
    local_rows = tokens.shape[0]
    capacity = local_rows * TOP // experts_cold
    is_hot, cold_rank, hot_match = slot_table(hot_list, experts_all)
    chosen, weight, shares = route_weights(routes, gate_q, experts_all)
    placed = jnp.cumsum(chosen, axis=0) - 1
    slot_hit = (
        (placed[:, :, None] == jnp.arange(capacity, dtype=jnp.int32)[None, None, :])
        & (chosen[:, :, None] > 0)
    ).astype(jnp.bfloat16)
    target = (
        (cold_rank[None, :] == jnp.arange(experts_cold, dtype=jnp.int32)[:, None])
        & (is_hot[None, :] == 0)
    ).astype(jnp.bfloat16)
    scatter_plan = jnp.einsum(
        "de,rec->dcr", target, slot_hit, preferred_element_type=jnp.float32
    ).astype(jnp.bfloat16)
    outgoing = jnp.einsum(
        "dcr,rk->dck", scatter_plan, tokens, preferred_element_type=jnp.float32
    ).astype(jnp.bfloat16)
    route_hot = jnp.take(is_hot, routes, axis=0)
    route_rank = jnp.take(cold_rank, routes, axis=0)
    route_place = jnp.take_along_axis(placed, routes, axis=1)
    flat_index = jnp.where(route_hot > 0, 0, route_rank * capacity + route_place)
    cold_share = jnp.where(route_hot > 0, jnp.float32(0.0), shares)
    hot_weight = jnp.sum(weight[:, None, :] * hot_match[None, :, :].astype(jnp.float32), axis=2)
    hot_paired = jnp.einsum(
        "rn,hgnf->hgrf",
        lax.all_gather(tokens, "tensor", axis=1, tiled=True),
        hot_gate_up,
        preferred_element_type=jnp.float32,
    )
    hot_hidden = (jax.nn.silu(hot_paired[:, 0]) * hot_paired[:, 1]).astype(jnp.bfloat16)
    hot_part = jnp.einsum("hrf,hfd->hrd", hot_hidden, hot_down, preferred_element_type=jnp.float32)
    hot_answer = lax.psum_scatter(
        hot_part.astype(jnp.bfloat16), "tensor", scatter_dimension=2, tiled=True
    )
    hot_total = jnp.sum(
        jnp.transpose(hot_weight)[:, :, None] * hot_answer.astype(jnp.float32), axis=0
    )
    widened = lax.all_gather(
        lax.all_to_all(outgoing, "expert", split_axis=0, concat_axis=0, tiled=True),
        "tensor",
        axis=2,
        tiled=True,
    )
    partial_out = swiglu(widened, cold_gate_up[0], cold_down[0])
    answers = lax.psum_scatter(partial_out, "tensor", scatter_dimension=2, tiled=True).astype(
        jnp.bfloat16
    )
    returned = lax.all_to_all(answers, "expert", split_axis=0, concat_axis=0, tiled=True)
    feature_part = returned.shape[2]
    flat_answers = returned.reshape(experts_cold * capacity, feature_part)
    picked_rows = jnp.take(flat_answers, flat_index.reshape(-1), axis=0).reshape(
        local_rows, TOP, feature_part
    )
    cold_total = jnp.sum(cold_share[:, :, None] * picked_rows.astype(jnp.float32), axis=1)
    return (cold_total + hot_total).astype(jnp.bfloat16)


def solution(mesh):
    meshes = mesh.shape["tensor"] == 1 and mesh.shape["expert"] == NZ * NY * NC
    return jax.shard_map(
        meshed if meshes else local,
        mesh=mesh,
        in_specs=(
            P(("group", "expert"), "tensor"),
            P(("group", "expert"), None),
            P(("group", "expert"), None),
            P(),
            P("expert", None, None, "tensor"),
            P("expert", "tensor", None),
            P(None, None, None, "tensor"),
            P(None, "tensor", None),
        ),
        out_specs=P(("group", "expert"), "tensor"),
        check_vma=False,
    )
```

```python
import functools

import jax
import jax.numpy as jnp
from jax import lax
from jax.experimental import pallas as pl
from jax.experimental.pallas import tpu as pltpu
from jax.sharding import PartitionSpec as P

TOP = 8
HOT = 1
NZ, NY, NC = 4, 2, 2
LANES = 128
F32 = jnp.float32
BF16 = jnp.bfloat16


def place():
    e = lax.axis_index("expert")
    return e // (NY * NC), (e // NC) % NY, e % NC


def index(z, y, c):
    return (z * NY + y) * NC + c


def greet(z, y, c):
    barrier = pltpu.get_barrier_semaphore()

    def hello(dev):
        pl.semaphore_signal(
            barrier, inc=1, device_id={"expert": dev}, device_id_type=pl.DeviceIdType.MESH
        )

    hello(index(z, y, 1 - c))
    hello(index(z, 1 - y, c))

    @pl.when(z > 0)
    def _():
        hello(index(z - 1, y, c))

    @pl.when(z < NZ - 1)
    def _():
        hello(index(z + 1, y, c))

    ends = (z == 0) | (z == NZ - 1)

    @pl.when(ends)
    def _():
        pl.semaphore_wait(barrier, 3)

    @pl.when(jnp.logical_not(ends))
    def _():
        pl.semaphore_wait(barrier, 4)


def spread_kernel(first, x_ref, out_ref, own_sem, send_sem, recv_sem):
    z, y, c = place()
    rows = x_ref.shape[0]
    half = first // 32 * 16
    parts = (pl.ds(0, half), pl.ds(half, first - half), pl.ds(first, rows - first))
    late = 2
    up, down, side, core = 0, 1, 2, 3
    own = index(z, y, c)
    keep = pltpu.make_async_copy(x_ref, out_ref.at[own], own_sem)
    keep.start()
    greet(z, y, c)

    def copy(way, source, part, from_input=False):
        target = (index(z + 1, y, c), index(z - 1, y, c), index(z, 1 - y, c), index(z, y, 1 - c))[way]
        block = x_ref if from_input else out_ref.at[source]
        return pltpu.make_async_remote_copy(
            src_ref=block.at[parts[part]],
            dst_ref=out_ref.at[source, parts[part]],
            send_sem=send_sem.at[way, source, part],
            recv_sem=recv_sem.at[source, part],
            device_id={"expert": target},
            device_id_type=pl.DeviceIdType.MESH,
        )

    def send(way, source, part, go=None, from_input=False):
        if go is None:
            copy(way, source, part, from_input).start()
        else:
            pl.when(go)(lambda: copy(way, source, part, from_input).start())

    def arrived(source, part):
        copy(core, source, part).wait_recv()

    def sent(way, source, part, go=None):
        if go is None:
            copy(way, source, part).wait_send()
        else:
            pl.when(go)(lambda: copy(way, source, part).wait_send())

    has_up, has_down = z < NZ - 1, z > 0
    beside = index(z, 1 - y, c)
    for part in (late, 0, 1):
        send(up, own, part, has_up, True)
        send(down, own, part, has_down, True)
        send(side, own, part, None, True)
    for part in (0, 1, late):
        send(core, own, part, None, True)
    arrived(beside, late)
    send(up, beside, late, has_up)
    send(down, beside, late, has_down)
    send(core, beside, late)

    def step(k, finish):
        for way in (up, down):
            zs = z - k if way == up else z + k
            there = (zs >= 0) if way == up else (zs < NZ)
            onward = has_up if way == up else has_down

            @pl.when(there)
            def _():
                mine, other = index(zs, y, c), index(zs, 1 - y, c)
                order = ((mine, late), (mine, 0), (mine, 1), (other, late))
                for source, part in order:
                    if finish:
                        sent(way, source, part, onward)
                        sent(core, source, part)
                    else:
                        arrived(source, part)
                        send(way, source, part, onward)
                        if part != late and source is mine:
                            send(side, source, part)
                        send(core, source, part)
                if finish:
                    sent(side, mine, 0)
                    sent(side, mine, 1)

    def cross(k, finish):
        for zs, there in ((z - k, z - k >= 0), (z + k, z + k < NZ)):

            @pl.when(there)
            def _():
                other = index(zs, 1 - y, c)
                for part in (0, 1):
                    if finish:
                        sent(core, other, part)
                    else:
                        arrived(other, part)
                        send(core, other, part)

    for k in range(1, NZ):
        step(k, False)
        if k == 1:
            for part in (0, 1):
                arrived(beside, part)
                send(core, beside, part)
        else:
            cross(k - 1, False)
    cross(NZ - 1, False)
    for zs in range(NZ):
        for ys in range(NY):
            for part in (0, 1, late):
                arrived(index(zs, ys, 1 - c), part)
    for part in (0, 1, late):
        sent(up, own, part, has_up)
        sent(down, own, part, has_down)
        sent(side, own, part)
        sent(core, own, part)
        sent(core, beside, part)
    sent(up, beside, late, has_up)
    sent(down, beside, late, has_down)
    for k in range(1, NZ):
        step(k, True)
        cross(k, True)
    keep.wait()


def spread(x, first):
    n = NZ * NY * NC
    return pl.pallas_call(
        functools.partial(spread_kernel, first),
        out_shape=jax.ShapeDtypeStruct((n,) + x.shape, x.dtype),
        in_specs=[pl.BlockSpec(memory_space=pl.ANY)],
        out_specs=pl.BlockSpec(memory_space=pl.ANY),
        scratch_shapes=[
            pltpu.SemaphoreType.DMA,
            pltpu.SemaphoreType.DMA((4, n, 3)),
            pltpu.SemaphoreType.DMA((n, 3)),
        ],
        compiler_params=pltpu.CompilerParams(collective_id=0, has_side_effects=True),
    )(x)


def fold_kernel(
    first, hid_ref, w_ref, hit_ref, share_ref, hot_ref, o_ref, p_ref, core_in, side_a, side_b, line_a, line_b, out_ya, out_yb, out_za, out_zb,
    core_s, core_r, ya_s, ya_r, yb_s, yb_r, za_s, za_r, zb_s, zb_r,
):
    z, y, c = place()
    rows = o_ref.shape[0]
    part_a, part_b = (0, first), (first, rows - first)
    greet(z, y, c)

    def remote(src, dst, s, r, target):
        return pltpu.make_async_remote_copy(
            src_ref=src, dst_ref=dst, send_sem=s, recv_sem=r,
            device_id={"expert": target}, device_id_type=pl.DeviceIdType.MESH,
        )

    def core_copy(zd, yd):
        return remote(p_ref.at[index(zd, yd, 1 - c)], core_in.at[zd, yd], core_s.at[zd, yd], core_r.at[zd, yd], index(z, y, 1 - c))

    def ya_copy(zd):
        return remote(out_ya.at[zd], side_a.at[zd], ya_s.at[zd], ya_r.at[zd], index(z, 1 - y, c))

    def yb_copy():
        return remote(out_yb, side_b, yb_s, yb_r, index(z, 1 - y, c))

    def za_copy(way, zd):
        return remote(out_za.at[zd], line_a.at[way, zd], za_s.at[zd], za_r.at[way, zd], index(z + 1 - 2 * way, y, c))

    def zb_copy(way, zd, yd):
        return remote(out_zb.at[zd, yd], line_b.at[way, zd, yd], zb_s.at[zd, yd], zb_r.at[way, zd, yd], index(z + 1 - 2 * way, y, c))

    def add(dst, part, *sources):
        def one(i, carry):
            at = pl.multiple_of(i * 16, 16)
            total = sources[0][0][pl.ds(sources[0][1] + at, 16), :].astype(F32)
            for ref, start in sources[1:]:
                total = total + ref[pl.ds(start + at, 16), :].astype(F32)
            dst[0][pl.ds(dst[1] + at, 16), :] = total.astype(dst[0].dtype)
            return carry

        lax.fori_loop(0, part[1] // 16, one, 0)

    def each(k, f):
        if k == 0:
            f(z, None)
        else:
            pl.when(z + k < NZ)(lambda: f(z + k, 0))
            pl.when(z - k >= 0)(lambda: f(z - k, 1))

    def produce(zd, way):
        width, tile = o_ref.shape[1], 512
        cap = hit_ref.shape[2]

        def one(t, carry):
            cols = pl.ds(pl.multiple_of(t * tile, tile), tile)
            answers = jnp.dot(hid_ref[zd], w_ref[:, cols], preferred_element_type=F32).astype(BF16)
            for b in range(NY * NC):
                mine = answers[b * cap : (b + 1) * cap]
                at = zd * (NY * NC) + b
                part = jnp.dot(hit_ref[at], mine, preferred_element_type=F32)
                p_ref[at, :, cols] = (part * share_ref[at][:, :1]).astype(BF16)
            return carry

        lax.fori_loop(0, width // tile, one, 0)
        for yd in range(NY):
            core_copy(zd, yd).start()

    def over_core(zd, way):
        core_copy(zd, 1 - y).wait_recv()
        add((out_ya.at[zd], 0), part_a, (p_ref.at[index(zd, 1 - y, c)], 0), (core_in.at[zd, 1 - y], 0))
        ya_copy(zd).start()
        core_copy(zd, y).wait_recv()

    def along(zd, way):
        first_of_line = (z == 0) if way == 0 else (z == NZ - 1)

        for yd in range(NY):
            base = ((p_ref.at[index(zd, yd, c)], first), (core_in.at[zd, yd], first))

            @pl.when(first_of_line)
            def _():
                add((out_zb.at[zd, yd], 0), part_b, *base)

            @pl.when(jnp.logical_not(first_of_line))
            def _():
                zb_copy(way, zd, yd).wait_recv()
                add((out_zb.at[zd, yd], 0), part_b, *base, (line_b.at[way, zd, yd], 0))

            zb_copy(way, zd, yd).start()
        ya_copy(zd).wait_recv()
        base = ((p_ref.at[index(zd, y, c)], 0), (core_in.at[zd, y], 0), (side_a.at[zd], 0))

        @pl.when(first_of_line)
        def _():
            add((out_za.at[zd], 0), part_a, *base)

        @pl.when(jnp.logical_not(first_of_line))
        def _():
            za_copy(way, zd).wait_recv()
            add((out_za.at[zd], 0), part_a, *base, (line_a.at[way, zd], 0))

        za_copy(way, zd).start()

    def finish(zd):
        def by_end(f):
            pl.when(z == 0)(lambda: f((1,)))
            pl.when(z == NZ - 1)(lambda: f((0,)))
            pl.when((z > 0) & (z < NZ - 1))(lambda: f((0, 1)))

        def last_b(ways):
            for yd, dst in ((1 - y, out_yb), (y, None)):
                for way in ways:
                    zb_copy(way, zd, yd).wait_recv()
                base = ((p_ref.at[index(zd, yd, c)], first), (core_in.at[zd, yd], first)) + tuple(
                    (line_b.at[way, zd, yd], 0) for way in ways
                )
                if dst is None:
                    yb_copy().wait_recv()
                    add((o_ref, first), part_b, *base, (side_b, 0), (hot_ref, first))
                else:
                    add((dst, 0), part_b, *base)
                    yb_copy().start()

        def last_a(ways):
            for way in ways:
                za_copy(way, zd).wait_recv()
            add(
                (o_ref, 0), part_a, (p_ref.at[index(zd, y, c)], 0), (core_in.at[zd, y], 0), (side_a.at[zd], 0),
                (hot_ref, 0), *((line_a.at[way, zd], 0) for way in ways),
            )

        ya_copy(zd).wait_recv()
        by_end(last_b)
        by_end(last_a)

    def drain(zd, way):
        for yd in range(NY):
            core_copy(zd, yd).wait_send()
        ya_copy(zd).wait_send()
        if way is None:
            yb_copy().wait_send()
        else:
            za_copy(way, zd).wait_send()
            for yd in range(NY):
                zb_copy(way, zd, yd).wait_send()

    each(3, produce)
    each(2, produce)
    each(3, over_core)
    each(1, produce)
    each(2, over_core)
    each(3, along)
    each(0, produce)
    each(1, over_core)
    each(2, along)
    each(0, over_core)
    each(1, along)
    finish(z)
    for k in (3, 2, 1, 0):
        each(k, drain)


def fold(hidden, down, hit, share, hot, first):
    n, rows = hit.shape[:2]
    width = down.shape[1]
    rest = rows - first
    dma = pltpu.SemaphoreType.DMA
    return pl.pallas_call(
        functools.partial(fold_kernel, first),
        out_shape=jax.ShapeDtypeStruct((rows, width), BF16),
        in_specs=[pl.BlockSpec(memory_space=pltpu.VMEM)] * 5,
        out_specs=pl.BlockSpec(memory_space=pltpu.VMEM),
        scratch_shapes=[
            pltpu.VMEM((n, rows, width), BF16),
            pltpu.VMEM((NZ, NY, rows, width), BF16),
            pltpu.VMEM((NZ, first, width), BF16),
            pltpu.VMEM((rest, width), BF16),
            pltpu.VMEM((2, NZ, first, width), BF16),
            pltpu.VMEM((2, NZ, NY, rest, width), BF16),
            pltpu.VMEM((NZ, first, width), BF16),
            pltpu.VMEM((rest, width), BF16),
            pltpu.VMEM((NZ, first, width), BF16),
            pltpu.VMEM((NZ, NY, rest, width), BF16),
            dma((NZ, NY)), dma((NZ, NY)),
            dma((NZ,)), dma((NZ,)),
            dma, dma,
            dma((NZ,)), dma((2, NZ)),
            dma((NZ, NY)), dma((2, NZ, NY)),
        ],
        compiler_params=pltpu.CompilerParams(
            collective_id=1, has_side_effects=True, vmem_limit_bytes=60 * 2**20
        ),
    )(hidden, down, hit, share, hot)


def meshed(tokens, routes, gate_q, hot_list, cold_gate_up, cold_down, hot_gate_up, hot_down):
    n = lax.axis_size("expert")
    rows, width = tokens.shape
    capacity = rows * TOP // n
    first = rows - 16
    is_hot, cold_rank, hot_match = slot_table(hot_list, n + HOT)
    picked = routes[:, :, None] == jnp.arange(n + HOT, dtype=jnp.int32)[None, None, :]
    by_label = jnp.sum(jnp.where(picked, gate_q[:, :, None], 0), axis=1)
    to_slot = jnp.where(is_hot > 0, n, cold_rank)
    slot_of = to_slot[:, None] == jnp.arange(n + 1, dtype=jnp.int32)[None, :]
    by_slot = jnp.sum(jnp.where(slot_of[None], by_label[:, :, None], 0), axis=1)
    whole = jnp.sum(gate_q, axis=1, keepdims=True)
    extra = jnp.concatenate([by_slot[:, :n], whole // 256, whole % 256], axis=1).astype(BF16)
    extra = jnp.pad(extra, ((0, 0), (0, LANES - extra.shape[1])))
    everything = spread(jnp.concatenate([tokens, extra], axis=1), first)

    notes = everything[:, :, width:].astype(F32)
    slot = lax.axis_index("expert")
    gate = jnp.sum(jnp.where(jnp.arange(LANES) == slot, notes, 0.0), axis=2)
    total = notes[:, :, n] * 256.0 + notes[:, :, n + 1]
    share = gate / total
    taken = gate > 0
    rank = jnp.cumsum(taken.astype(jnp.int32), axis=1) - 1
    hit = (rank[:, :, None] == jnp.arange(capacity, dtype=jnp.int32)) & taken[:, :, None]
    hit = hit.astype(BF16)
    x = jnp.einsum("brc,brd->bcd", hit, everything[:, :, :width], preferred_element_type=F32)
    x = x.astype(BF16).reshape(n * capacity, width)
    hidden = hidden_of(x, cold_gate_up[0]).reshape(NZ, -1, cold_gate_up.shape[3])
    share = jnp.broadcast_to(share[:, :, None], share.shape + (LANES,))

    hot_share = by_slot[:, n:].astype(F32) / whole.astype(F32)
    hot = hot_share * expert(tokens, hot_gate_up[0], hot_down[0]).astype(F32)
    return fold(hidden, cold_down[0], hit, share, hot, first)


def hidden_of(x, gate_up):
    paired = jnp.einsum("nd,gdf->gnf", x, gate_up, preferred_element_type=F32)
    return (jax.nn.silu(paired[0]) * paired[1]).astype(BF16)


def expert(x, gate_up, down):
    return jnp.einsum("nf,fd->nd", hidden_of(x, gate_up), down, preferred_element_type=F32).astype(BF16)


def slot_table(hot_list, experts_all):
    labels = jnp.arange(experts_all, dtype=jnp.int32)
    hot_match = (hot_list[:, None] == labels[None, :]).astype(jnp.int32)
    is_hot = jnp.sum(hot_match, axis=0)
    cold_rank = jnp.cumsum(1 - is_hot) - 1
    return (is_hot, cold_rank, hot_match)


def route_weights(routes, gate_q, experts_all):
    quantized = gate_q.astype(jnp.float32)
    shares = quantized / jnp.sum(quantized, axis=1, keepdims=True)
    labels = jnp.arange(experts_all, dtype=jnp.int32)
    picked = routes[:, :, None] == labels[None, None, :]
    chosen = jnp.sum(picked.astype(jnp.int32), axis=1)
    weight = jnp.sum(jnp.where(picked, shares[:, :, None], jnp.float32(0.0)), axis=1)
    return (chosen, weight, shares)


def swiglu(inputs, gate_up, down_proj):
    paired = jnp.einsum("snd,gdf->gsnf", inputs, gate_up, preferred_element_type=jnp.float32)
    hidden = (jax.nn.silu(paired[0]) * paired[1]).astype(jnp.bfloat16)
    return jnp.einsum("snf,fd->snd", hidden, down_proj, preferred_element_type=jnp.float32)


def local(tokens, routes, gate_q, hot_list, cold_gate_up, cold_down, hot_gate_up, hot_down):
    experts_cold = lax.axis_size("expert")
    experts_all = experts_cold + HOT
    local_rows = tokens.shape[0]
    capacity = local_rows * TOP // experts_cold
    is_hot, cold_rank, hot_match = slot_table(hot_list, experts_all)
    chosen, weight, shares = route_weights(routes, gate_q, experts_all)
    placed = jnp.cumsum(chosen, axis=0) - 1
    slot_hit = (
        (placed[:, :, None] == jnp.arange(capacity, dtype=jnp.int32)[None, None, :])
        & (chosen[:, :, None] > 0)
    ).astype(jnp.bfloat16)
    target = (
        (cold_rank[None, :] == jnp.arange(experts_cold, dtype=jnp.int32)[:, None])
        & (is_hot[None, :] == 0)
    ).astype(jnp.bfloat16)
    scatter_plan = jnp.einsum(
        "de,rec->dcr", target, slot_hit, preferred_element_type=jnp.float32
    ).astype(jnp.bfloat16)
    outgoing = jnp.einsum(
        "dcr,rk->dck", scatter_plan, tokens, preferred_element_type=jnp.float32
    ).astype(jnp.bfloat16)
    route_hot = jnp.take(is_hot, routes, axis=0)
    route_rank = jnp.take(cold_rank, routes, axis=0)
    route_place = jnp.take_along_axis(placed, routes, axis=1)
    flat_index = jnp.where(route_hot > 0, 0, route_rank * capacity + route_place)
    cold_share = jnp.where(route_hot > 0, jnp.float32(0.0), shares)
    hot_weight = jnp.sum(weight[:, None, :] * hot_match[None, :, :].astype(jnp.float32), axis=2)
    hot_paired = jnp.einsum(
        "rn,hgnf->hgrf",
        lax.all_gather(tokens, "tensor", axis=1, tiled=True),
        hot_gate_up,
        preferred_element_type=jnp.float32,
    )
    hot_hidden = (jax.nn.silu(hot_paired[:, 0]) * hot_paired[:, 1]).astype(jnp.bfloat16)
    hot_part = jnp.einsum("hrf,hfd->hrd", hot_hidden, hot_down, preferred_element_type=jnp.float32)
    hot_answer = lax.psum_scatter(
        hot_part.astype(jnp.bfloat16), "tensor", scatter_dimension=2, tiled=True
    )
    hot_total = jnp.sum(
        jnp.transpose(hot_weight)[:, :, None] * hot_answer.astype(jnp.float32), axis=0
    )
    widened = lax.all_gather(
        lax.all_to_all(outgoing, "expert", split_axis=0, concat_axis=0, tiled=True),
        "tensor",
        axis=2,
        tiled=True,
    )
    partial_out = swiglu(widened, cold_gate_up[0], cold_down[0])
    answers = lax.psum_scatter(partial_out, "tensor", scatter_dimension=2, tiled=True).astype(
        jnp.bfloat16
    )
    returned = lax.all_to_all(answers, "expert", split_axis=0, concat_axis=0, tiled=True)
    feature_part = returned.shape[2]
    flat_answers = returned.reshape(experts_cold * capacity, feature_part)
    picked_rows = jnp.take(flat_answers, flat_index.reshape(-1), axis=0).reshape(
        local_rows, TOP, feature_part
    )
    cold_total = jnp.sum(cold_share[:, :, None] * picked_rows.astype(jnp.float32), axis=1)
    return (cold_total + hot_total).astype(jnp.bfloat16)


def solution(mesh):
    meshes = mesh.shape["tensor"] == 1 and mesh.shape["expert"] == NZ * NY * NC
    return jax.shard_map(
        meshed if meshes else local,
        mesh=mesh,
        in_specs=(
            P(("group", "expert"), "tensor"),
            P(("group", "expert"), None),
            P(("group", "expert"), None),
            P(),
            P("expert", None, None, "tensor"),
            P("expert", "tensor", None),
            P(None, None, None, "tensor"),
            P(None, "tensor", None),
        ),
        out_specs=P(("group", "expert"), "tensor"),
        check_vma=False,
    )
```

```python
import functools

import jax
import jax.numpy as jnp
from jax import lax
from jax.experimental import pallas as pl
from jax.experimental.pallas import tpu as pltpu
from jax.sharding import PartitionSpec as P

TOP = 8
HOT = 1
NZ, NY, NC = 4, 2, 2
LANES = 128
F32 = jnp.float32
BF16 = jnp.bfloat16


def place():
    e = lax.axis_index("expert")
    return e // (NY * NC), (e // NC) % NY, e % NC


def index(z, y, c):
    return (z * NY + y) * NC + c


def greet(z, y, c):
    barrier = pltpu.get_barrier_semaphore()

    def hello(dev):
        pl.semaphore_signal(
            barrier, inc=1, device_id={"expert": dev}, device_id_type=pl.DeviceIdType.MESH
        )

    hello(index(z, y, 1 - c))
    hello(index(z, 1 - y, c))

    @pl.when(z > 0)
    def _():
        hello(index(z - 1, y, c))

    @pl.when(z < NZ - 1)
    def _():
        hello(index(z + 1, y, c))

    ends = (z == 0) | (z == NZ - 1)

    @pl.when(ends)
    def _():
        pl.semaphore_wait(barrier, 3)

    @pl.when(jnp.logical_not(ends))
    def _():
        pl.semaphore_wait(barrier, 4)


def spread_kernel(
    first, x_ref, gu_ref, dn_ref, out_ref, hot_ref, x_in, gu_in, dn_in, mid, own_sem, load_sem, send_sem, recv_sem
):
    z, y, c = place()
    rows = x_ref.shape[0]
    half = first // 32 * 16
    parts = (pl.ds(0, half), pl.ds(half, first - half), pl.ds(first, rows - first))
    late = 2
    up, down, side, core = 0, 1, 2, 3
    own = index(z, y, c)
    keep = pltpu.make_async_copy(x_ref, out_ref.at[own], own_sem)
    keep.start()
    loads = [
        pltpu.make_async_copy(src, dst, load_sem.at[i])
        for i, (src, dst) in enumerate(((x_ref, x_in), (gu_ref, gu_in), (dn_ref, dn_in)))
    ]
    for load in loads:
        load.start()
    greet(z, y, c)

    def copy(way, source, part, from_input=False):
        target = (index(z + 1, y, c), index(z - 1, y, c), index(z, 1 - y, c), index(z, y, 1 - c))[way]
        block = x_ref if from_input else out_ref.at[source]
        return pltpu.make_async_remote_copy(
            src_ref=block.at[parts[part]],
            dst_ref=out_ref.at[source, parts[part]],
            send_sem=send_sem.at[way, source, part],
            recv_sem=recv_sem.at[source, part],
            device_id={"expert": target},
            device_id_type=pl.DeviceIdType.MESH,
        )

    def send(way, source, part, go=None, from_input=False):
        if go is None:
            copy(way, source, part, from_input).start()
        else:
            pl.when(go)(lambda: copy(way, source, part, from_input).start())

    def arrived(source, part):
        copy(core, source, part).wait_recv()

    def sent(way, source, part, go=None):
        if go is None:
            copy(way, source, part).wait_send()
        else:
            pl.when(go)(lambda: copy(way, source, part).wait_send())

    has_up, has_down = z < NZ - 1, z > 0
    beside = index(z, 1 - y, c)
    for part in (late, 0, 1):
        send(up, own, part, has_up, True)
        send(down, own, part, has_down, True)
        send(side, own, part, None, True)
    for part in (0, 1, late):
        send(core, own, part, None, True)
    arrived(beside, late)
    send(up, beside, late, has_up)
    send(down, beside, late, has_down)
    send(core, beside, late)

    def step(k, finish):
        for way in (up, down):
            zs = z - k if way == up else z + k
            there = (zs >= 0) if way == up else (zs < NZ)
            onward = has_up if way == up else has_down

            @pl.when(there)
            def _():
                mine, other = index(zs, y, c), index(zs, 1 - y, c)
                order = ((mine, late), (mine, 0), (mine, 1), (other, late))
                for source, part in order:
                    if finish:
                        sent(way, source, part, onward)
                        sent(core, source, part)
                    else:
                        arrived(source, part)
                        send(way, source, part, onward)
                        if part != late and source is mine:
                            send(side, source, part)
                        send(core, source, part)
                if finish:
                    sent(side, mine, 0)
                    sent(side, mine, 1)

    def cross(k, finish):
        for zs, there in ((z - k, z - k >= 0), (z + k, z + k < NZ)):

            @pl.when(there)
            def _():
                other = index(zs, 1 - y, c)
                for part in (0, 1):
                    if finish:
                        sent(core, other, part)
                    else:
                        arrived(other, part)
                        send(core, other, part)

    def hot_expert():
        for load in loads:
            load.wait()
        tile, depth = 256, gu_in.shape[1]

        def paired(t, carry):
            cols = pl.ds(pl.multiple_of(t * tile, tile), tile)
            gate = jnp.dot(x_in[:, :depth], gu_in[0, :, cols], preferred_element_type=F32)
            up_ = jnp.dot(x_in[:, :depth], gu_in[1, :, cols], preferred_element_type=F32)
            mid[:, cols] = (jax.nn.silu(gate) * up_).astype(BF16)
            return carry

        lax.fori_loop(0, gu_in.shape[2] // tile, paired, 0)

        def answer(t, carry):
            cols = pl.ds(pl.multiple_of(t * tile, tile), tile)
            hot_ref[:, cols] = jnp.dot(mid[...], dn_in[:, cols], preferred_element_type=F32).astype(BF16)
            return carry

        lax.fori_loop(0, depth // tile, answer, 0)

    for k in range(1, NZ):
        step(k, False)
        if k == 1:
            hot_expert()
            for part in (0, 1):
                arrived(beside, part)
                send(core, beside, part)
        else:
            cross(k - 1, False)
    cross(NZ - 1, False)
    for zs in range(NZ):
        for ys in range(NY):
            for part in (0, 1, late):
                arrived(index(zs, ys, 1 - c), part)
    for part in (0, 1, late):
        sent(up, own, part, has_up)
        sent(down, own, part, has_down)
        sent(side, own, part)
        sent(core, own, part)
        sent(core, beside, part)
    sent(up, beside, late, has_up)
    sent(down, beside, late, has_down)
    for k in range(1, NZ):
        step(k, True)
        cross(k, True)
    keep.wait()


def spread(x, gate_up, down, first):
    n = NZ * NY * NC
    return pl.pallas_call(
        functools.partial(spread_kernel, first),
        out_shape=[
            jax.ShapeDtypeStruct((n,) + x.shape, x.dtype),
            jax.ShapeDtypeStruct((x.shape[0], down.shape[1]), BF16),
        ],
        in_specs=[pl.BlockSpec(memory_space=pl.ANY)] * 3,
        out_specs=[pl.BlockSpec(memory_space=pl.ANY), pl.BlockSpec(memory_space=pltpu.VMEM)],
        scratch_shapes=[
            pltpu.VMEM(x.shape, BF16),
            pltpu.VMEM(gate_up.shape, BF16),
            pltpu.VMEM(down.shape, BF16),
            pltpu.VMEM((x.shape[0], down.shape[0]), BF16),
            pltpu.SemaphoreType.DMA,
            pltpu.SemaphoreType.DMA((3,)),
            pltpu.SemaphoreType.DMA((4, n, 3)),
            pltpu.SemaphoreType.DMA((n, 3)),
        ],
        compiler_params=pltpu.CompilerParams(
            collective_id=0, has_side_effects=True, vmem_limit_bytes=48 * 2**20
        ),
    )(x, gate_up, down)


def fold_kernel(
    first, hid_ref, w_ref, hit_ref, share_ref, hot_ref, o_ref, p_ref, core_in, side_a, side_b, line_a, line_b, out_ya, out_yb, out_za, out_zb,
    core_s, core_r, ya_s, ya_r, yb_s, yb_r, za_s, za_r, zb_s, zb_r,
):
    z, y, c = place()
    rows = o_ref.shape[0]
    part_a, part_b = (0, first), (first, rows - first)
    greet(z, y, c)

    def remote(src, dst, s, r, target):
        return pltpu.make_async_remote_copy(
            src_ref=src, dst_ref=dst, send_sem=s, recv_sem=r,
            device_id={"expert": target}, device_id_type=pl.DeviceIdType.MESH,
        )

    def core_copy(zd, yd):
        return remote(p_ref.at[index(zd, yd, 1 - c)], core_in.at[zd, yd], core_s.at[zd, yd], core_r.at[zd, yd], index(z, y, 1 - c))

    def ya_copy(zd):
        return remote(out_ya.at[zd], side_a.at[zd], ya_s.at[zd], ya_r.at[zd], index(z, 1 - y, c))

    def yb_copy():
        return remote(out_yb, side_b, yb_s, yb_r, index(z, 1 - y, c))

    def za_copy(way, zd):
        return remote(out_za.at[zd], line_a.at[way, zd], za_s.at[zd], za_r.at[way, zd], index(z + 1 - 2 * way, y, c))

    def zb_copy(way, zd, yd):
        return remote(out_zb.at[zd, yd], line_b.at[way, zd, yd], zb_s.at[zd, yd], zb_r.at[way, zd, yd], index(z + 1 - 2 * way, y, c))

    def add(dst, part, *sources):
        def one(i, carry):
            at = pl.multiple_of(i * 16, 16)
            total = sources[0][0][pl.ds(sources[0][1] + at, 16), :].astype(F32)
            for ref, start in sources[1:]:
                total = total + ref[pl.ds(start + at, 16), :].astype(F32)
            dst[0][pl.ds(dst[1] + at, 16), :] = total.astype(dst[0].dtype)
            return carry

        lax.fori_loop(0, part[1] // 16, one, 0)

    def each(k, f):
        if k == 0:
            f(z, None)
        else:
            pl.when(z + k < NZ)(lambda: f(z + k, 0))
            pl.when(z - k >= 0)(lambda: f(z - k, 1))

    def produce(zd, way):
        width, tile = o_ref.shape[1], 512
        cap = hit_ref.shape[2]

        def one(t, carry):
            cols = pl.ds(pl.multiple_of(t * tile, tile), tile)
            answers = jnp.dot(hid_ref[zd], w_ref[:, cols], preferred_element_type=F32).astype(BF16)
            for b in range(NY * NC):
                mine = answers[b * cap : (b + 1) * cap]
                at = zd * (NY * NC) + b
                part = jnp.dot(hit_ref[at], mine, preferred_element_type=F32)
                p_ref[at, :, cols] = (part * share_ref[at][:, :1]).astype(BF16)
            return carry

        lax.fori_loop(0, width // tile, one, 0)
        for yd in range(NY):
            core_copy(zd, yd).start()

    def over_core(zd, way):
        core_copy(zd, 1 - y).wait_recv()
        add((out_ya.at[zd], 0), part_a, (p_ref.at[index(zd, 1 - y, c)], 0), (core_in.at[zd, 1 - y], 0))
        ya_copy(zd).start()
        core_copy(zd, y).wait_recv()

    def along(zd, way):
        first_of_line = (z == 0) if way == 0 else (z == NZ - 1)

        for yd in range(NY):
            base = ((p_ref.at[index(zd, yd, c)], first), (core_in.at[zd, yd], first))

            @pl.when(first_of_line)
            def _():
                add((out_zb.at[zd, yd], 0), part_b, *base)

            @pl.when(jnp.logical_not(first_of_line))
            def _():
                zb_copy(way, zd, yd).wait_recv()
                add((out_zb.at[zd, yd], 0), part_b, *base, (line_b.at[way, zd, yd], 0))

            zb_copy(way, zd, yd).start()
        ya_copy(zd).wait_recv()
        base = ((p_ref.at[index(zd, y, c)], 0), (core_in.at[zd, y], 0), (side_a.at[zd], 0))

        @pl.when(first_of_line)
        def _():
            add((out_za.at[zd], 0), part_a, *base)

        @pl.when(jnp.logical_not(first_of_line))
        def _():
            za_copy(way, zd).wait_recv()
            add((out_za.at[zd], 0), part_a, *base, (line_a.at[way, zd], 0))

        za_copy(way, zd).start()

    def finish(zd):
        def by_end(f):
            pl.when(z == 0)(lambda: f((1,)))
            pl.when(z == NZ - 1)(lambda: f((0,)))
            pl.when((z > 0) & (z < NZ - 1))(lambda: f((0, 1)))

        def last_b(ways):
            for yd, dst in ((1 - y, out_yb), (y, None)):
                for way in ways:
                    zb_copy(way, zd, yd).wait_recv()
                base = ((p_ref.at[index(zd, yd, c)], first), (core_in.at[zd, yd], first)) + tuple(
                    (line_b.at[way, zd, yd], 0) for way in ways
                )
                if dst is None:
                    yb_copy().wait_recv()
                    add((o_ref, first), part_b, *base, (side_b, 0), (hot_ref, first))
                else:
                    add((dst, 0), part_b, *base)
                    yb_copy().start()

        def last_a(ways):
            for way in ways:
                za_copy(way, zd).wait_recv()
            add(
                (o_ref, 0), part_a, (p_ref.at[index(zd, y, c)], 0), (core_in.at[zd, y], 0), (side_a.at[zd], 0),
                (hot_ref, 0), *((line_a.at[way, zd], 0) for way in ways),
            )

        ya_copy(zd).wait_recv()
        by_end(last_b)
        by_end(last_a)

    def drain(zd, way):
        for yd in range(NY):
            core_copy(zd, yd).wait_send()
        ya_copy(zd).wait_send()
        if way is None:
            yb_copy().wait_send()
        else:
            za_copy(way, zd).wait_send()
            for yd in range(NY):
                zb_copy(way, zd, yd).wait_send()

    each(3, produce)
    each(2, produce)
    each(3, over_core)
    each(1, produce)
    each(2, over_core)
    each(3, along)
    each(0, produce)
    each(1, over_core)
    each(2, along)
    each(0, over_core)
    each(1, along)
    finish(z)
    for k in (3, 2, 1, 0):
        each(k, drain)


def fold(hidden, down, hit, share, hot, first):
    n, rows = hit.shape[:2]
    width = down.shape[1]
    rest = rows - first
    dma = pltpu.SemaphoreType.DMA
    return pl.pallas_call(
        functools.partial(fold_kernel, first),
        out_shape=jax.ShapeDtypeStruct((rows, width), BF16),
        in_specs=[pl.BlockSpec(memory_space=pltpu.VMEM)] * 5,
        out_specs=pl.BlockSpec(memory_space=pltpu.VMEM),
        scratch_shapes=[
            pltpu.VMEM((n, rows, width), BF16),
            pltpu.VMEM((NZ, NY, rows, width), BF16),
            pltpu.VMEM((NZ, first, width), BF16),
            pltpu.VMEM((rest, width), BF16),
            pltpu.VMEM((2, NZ, first, width), BF16),
            pltpu.VMEM((2, NZ, NY, rest, width), BF16),
            pltpu.VMEM((NZ, first, width), BF16),
            pltpu.VMEM((rest, width), BF16),
            pltpu.VMEM((NZ, first, width), BF16),
            pltpu.VMEM((NZ, NY, rest, width), BF16),
            dma((NZ, NY)), dma((NZ, NY)),
            dma((NZ,)), dma((NZ,)),
            dma, dma,
            dma((NZ,)), dma((2, NZ)),
            dma((NZ, NY)), dma((2, NZ, NY)),
        ],
        compiler_params=pltpu.CompilerParams(
            collective_id=1, has_side_effects=True, vmem_limit_bytes=60 * 2**20
        ),
    )(hidden, down, hit, share, hot)


def meshed(tokens, routes, gate_q, hot_list, cold_gate_up, cold_down, hot_gate_up, hot_down):
    n = lax.axis_size("expert")
    rows, width = tokens.shape
    capacity = rows * TOP // n
    first = rows - 16
    is_hot, cold_rank, hot_match = slot_table(hot_list, n + HOT)
    picked = routes[:, :, None] == jnp.arange(n + HOT, dtype=jnp.int32)[None, None, :]
    by_label = jnp.sum(jnp.where(picked, gate_q[:, :, None], 0), axis=1)
    to_slot = jnp.where(is_hot > 0, n, cold_rank)
    slot_of = to_slot[:, None] == jnp.arange(n + 1, dtype=jnp.int32)[None, :]
    by_slot = jnp.sum(jnp.where(slot_of[None], by_label[:, :, None], 0), axis=1)
    whole = jnp.sum(gate_q, axis=1, keepdims=True)
    extra = jnp.concatenate([by_slot[:, :n], whole // 256, whole % 256], axis=1).astype(BF16)
    extra = jnp.pad(extra, ((0, 0), (0, LANES - extra.shape[1])))
    everything, hot_answer = spread(
        jnp.concatenate([tokens, extra], axis=1), hot_gate_up[0], hot_down[0], first
    )

    notes = everything[:, :, width:].astype(F32)
    slot = lax.axis_index("expert")
    gate = jnp.sum(jnp.where(jnp.arange(LANES) == slot, notes, 0.0), axis=2)
    total = notes[:, :, n] * 256.0 + notes[:, :, n + 1]
    share = gate / total
    taken = gate > 0
    rank = jnp.cumsum(taken.astype(jnp.int32), axis=1) - 1
    hit = (rank[:, :, None] == jnp.arange(capacity, dtype=jnp.int32)) & taken[:, :, None]
    hit = hit.astype(BF16)
    x = jnp.einsum("brc,brd->bcd", hit, everything[:, :, :width], preferred_element_type=F32)
    x = x.astype(BF16).reshape(n * capacity, width)
    hidden = hidden_of(x, cold_gate_up[0]).reshape(NZ, -1, cold_gate_up.shape[3])
    share = jnp.broadcast_to(share[:, :, None], share.shape + (LANES,))

    hot_share = by_slot[:, n:].astype(F32) / whole.astype(F32)
    hot = hot_share * hot_answer.astype(F32)
    return fold(hidden, cold_down[0], hit, share, hot, first)


def hidden_of(x, gate_up):
    paired = jnp.einsum("nd,gdf->gnf", x, gate_up, preferred_element_type=F32)
    return (jax.nn.silu(paired[0]) * paired[1]).astype(BF16)


def slot_table(hot_list, experts_all):
    labels = jnp.arange(experts_all, dtype=jnp.int32)
    hot_match = (hot_list[:, None] == labels[None, :]).astype(jnp.int32)
    is_hot = jnp.sum(hot_match, axis=0)
    cold_rank = jnp.cumsum(1 - is_hot) - 1
    return (is_hot, cold_rank, hot_match)


def route_weights(routes, gate_q, experts_all):
    quantized = gate_q.astype(jnp.float32)
    shares = quantized / jnp.sum(quantized, axis=1, keepdims=True)
    labels = jnp.arange(experts_all, dtype=jnp.int32)
    picked = routes[:, :, None] == labels[None, None, :]
    chosen = jnp.sum(picked.astype(jnp.int32), axis=1)
    weight = jnp.sum(jnp.where(picked, shares[:, :, None], jnp.float32(0.0)), axis=1)
    return (chosen, weight, shares)


def swiglu(inputs, gate_up, down_proj):
    paired = jnp.einsum("snd,gdf->gsnf", inputs, gate_up, preferred_element_type=jnp.float32)
    hidden = (jax.nn.silu(paired[0]) * paired[1]).astype(jnp.bfloat16)
    return jnp.einsum("snf,fd->snd", hidden, down_proj, preferred_element_type=jnp.float32)


def local(tokens, routes, gate_q, hot_list, cold_gate_up, cold_down, hot_gate_up, hot_down):
    experts_cold = lax.axis_size("expert")
    experts_all = experts_cold + HOT
    local_rows = tokens.shape[0]
    capacity = local_rows * TOP // experts_cold
    is_hot, cold_rank, hot_match = slot_table(hot_list, experts_all)
    chosen, weight, shares = route_weights(routes, gate_q, experts_all)
    placed = jnp.cumsum(chosen, axis=0) - 1
    slot_hit = (
        (placed[:, :, None] == jnp.arange(capacity, dtype=jnp.int32)[None, None, :])
        & (chosen[:, :, None] > 0)
    ).astype(jnp.bfloat16)
    target = (
        (cold_rank[None, :] == jnp.arange(experts_cold, dtype=jnp.int32)[:, None])
        & (is_hot[None, :] == 0)
    ).astype(jnp.bfloat16)
    scatter_plan = jnp.einsum(
        "de,rec->dcr", target, slot_hit, preferred_element_type=jnp.float32
    ).astype(jnp.bfloat16)
    outgoing = jnp.einsum(
        "dcr,rk->dck", scatter_plan, tokens, preferred_element_type=jnp.float32
    ).astype(jnp.bfloat16)
    route_hot = jnp.take(is_hot, routes, axis=0)
    route_rank = jnp.take(cold_rank, routes, axis=0)
    route_place = jnp.take_along_axis(placed, routes, axis=1)
    flat_index = jnp.where(route_hot > 0, 0, route_rank * capacity + route_place)
    cold_share = jnp.where(route_hot > 0, jnp.float32(0.0), shares)
    hot_weight = jnp.sum(weight[:, None, :] * hot_match[None, :, :].astype(jnp.float32), axis=2)
    hot_paired = jnp.einsum(
        "rn,hgnf->hgrf",
        lax.all_gather(tokens, "tensor", axis=1, tiled=True),
        hot_gate_up,
        preferred_element_type=jnp.float32,
    )
    hot_hidden = (jax.nn.silu(hot_paired[:, 0]) * hot_paired[:, 1]).astype(jnp.bfloat16)
    hot_part = jnp.einsum("hrf,hfd->hrd", hot_hidden, hot_down, preferred_element_type=jnp.float32)
    hot_answer = lax.psum_scatter(
        hot_part.astype(jnp.bfloat16), "tensor", scatter_dimension=2, tiled=True
    )
    hot_total = jnp.sum(
        jnp.transpose(hot_weight)[:, :, None] * hot_answer.astype(jnp.float32), axis=0
    )
    widened = lax.all_gather(
        lax.all_to_all(outgoing, "expert", split_axis=0, concat_axis=0, tiled=True),
        "tensor",
        axis=2,
        tiled=True,
    )
    partial_out = swiglu(widened, cold_gate_up[0], cold_down[0])
    answers = lax.psum_scatter(partial_out, "tensor", scatter_dimension=2, tiled=True).astype(
        jnp.bfloat16
    )
    returned = lax.all_to_all(answers, "expert", split_axis=0, concat_axis=0, tiled=True)
    feature_part = returned.shape[2]
    flat_answers = returned.reshape(experts_cold * capacity, feature_part)
    picked_rows = jnp.take(flat_answers, flat_index.reshape(-1), axis=0).reshape(
        local_rows, TOP, feature_part
    )
    cold_total = jnp.sum(cold_share[:, :, None] * picked_rows.astype(jnp.float32), axis=1)
    return (cold_total + hot_total).astype(jnp.bfloat16)


def solution(mesh):
    meshes = mesh.shape["tensor"] == 1 and mesh.shape["expert"] == NZ * NY * NC
    return jax.shard_map(
        meshed if meshes else local,
        mesh=mesh,
        in_specs=(
            P(("group", "expert"), "tensor"),
            P(("group", "expert"), None),
            P(("group", "expert"), None),
            P(),
            P("expert", None, None, "tensor"),
            P("expert", "tensor", None),
            P(None, None, None, "tensor"),
            P(None, "tensor", None),
        ),
        out_specs=P(("group", "expert"), "tensor"),
        check_vma=False,
    )
```
